32 devices in a mesh: groups: 2 (over y), tensor: 4 (over z), dp: 2 (over x), section: 2 (over core).
Axes of the slice: x: 2, y: 2, z: 4, core: 2. Of those that a mesh axis runs over, the one named last changes fastest.
Arguments:
- attended: bfloat16 [4, 4096, 4096], P(('groups', 'dp'), 'tensor', 'section'), parts along dimension 0, may hold values from -6 to 6
- weight_tiles: bfloat16 [4, 2, 256, 128, 128], P('tensor', 'section'), may hold values from -0.125 to 0.125
- block_lists: int32 [4, 2, 256], P('tensor', 'section'), may hold values from 0 to 255, as said below
- kept_counts: int32 [4, 2], P('tensor', 'section'), may hold values from 64 to 256, as said below
- out_grad: bfloat16 [4, 4096, 8192], P(('groups', 'dp'), None, ('tensor', 'section')), parts along dimension 0, may hold values from -6 to 6
Outputs:
- projected: bfloat16 [4, 4096, 8192], P(('groups', 'dp'), None, 'tensor'), parts along dimension 0
- tiles_grad: float32 [8, 2, 256, 128, 128], P(('groups', 'tensor'), 'section', 'dp'), parts along dimension 0
The draws below stay inside these ranges and needn't reach their ends.
There are 2 independent parts, one for each index of `groups`. The reference program is written for one: setup_inputs(seed, part) draws one part's arguments, and reference() takes and returns one part's arrays. A program takes and returns all parts, laid end to end along the dimension named above; an argument that names none is the same for every part. Nothing has to cross between parts.
Inputs may be any that keep to these rules, and one draw needn't show every extreme that they name: `kept_counts`: every shard keeps at least a quarter of its 256 blocks; some shard keeps all of them; on average about half are kept. `block_lists`: each shard's list names each of its 256 local blocks once; the first kept_counts entries are its kept blocks in increasing order, the rest its other blocks in increasing order.
All inputs are finite; a program needn't handle non-finite values.
Results may differ from the reference program's by a relative error of at most 0.009.
Values may be sent and summed in bfloat16 or wider, within the bound.
A program may use at most 192 MiB of HBM per device.

```python
import jax
import jax.numpy as jnp
from jax import lax

D = 8192
IN_W = 4096
BLK = 128
LEN = 4096
SEQS = 2
SLOTS = 256
N_TENSOR = 4
N_SECTION = 2


def kept_layout(key):
    count_key, full_key, order_key = jax.random.split(key, 3)
    shard_total = N_TENSOR * N_SECTION
    drawn = jax.random.randint(count_key, (shard_total,), SLOTS // 4, 3 * SLOTS // 4 + 1)
    full_shard = jax.random.randint(full_key, (), 0, shard_total)
    drawn = jnp.where(jnp.arange(shard_total) == full_shard, SLOTS, drawn).astype(jnp.int32)
    shard_keys = jax.random.split(order_key, shard_total)
    ranks = jax.vmap(lambda k: jnp.argsort(jax.random.permutation(k, SLOTS)))(shard_keys)
    kept = ranks < drawn[:, None]
    scores = jnp.where(kept, 0, SLOTS) + jnp.arange(SLOTS)[None, :]
    listing = jnp.argsort(scores, axis=1).astype(jnp.int32)
    return (drawn.reshape(N_TENSOR, N_SECTION), listing.reshape(N_TENSOR, N_SECTION, SLOTS))


def draw_block_lists(key, part):
    drawn, listing = kept_layout(key)
    return listing


def draw_kept_counts(key, part):
    drawn, listing = kept_layout(key)
    return drawn


def block_scale(rng, dims, shards, smallest, top_value):
    factor_of, own = 1.0, jax.random.fold_in(rng, 6)
    for dim, blocks in shards:
        heights = jnp.exp(jax.random.uniform(jax.random.fold_in(own, dim), (blocks,), jnp.float32, smallest / len(shards), top_value / len(shards)))
        factor_of = factor_of * jnp.repeat(heights, dims[dim] // blocks).reshape([-1 if axis == dim else 1 for axis in range(len(dims))])
    return factor_of


def noise(key, dims, width, limit, pieces=(), dtype=jnp.bfloat16):
    result = width * jax.random.normal(key, dims, jnp.float32)
    if pieces:
        result = result * block_scale(key, dims, pieces, -0.22, 0.18)
    return jnp.clip(result, -limit, limit).astype(dtype)


def setup_inputs(seed: int = 0, part: int = 0) -> dict:
    arg_keys = jax.random.split(jax.random.key(seed), 6)
    own_keys = jax.random.split(jax.random.fold_in(arg_keys[5], part), 6)
    attended = noise(own_keys[0], (SEQS, LEN, IN_W), 1.0, 6.0, ((0, 2), (1, 4), (2, 2)))
    weight_tiles = noise(arg_keys[1], (N_TENSOR, N_SECTION, SLOTS, BLK, BLK), (IN_W // 2) ** -0.5, 0.125, ((0, 4), (1, 2)))
    block_lists = draw_block_lists(jax.random.fold_in(arg_keys[5], 71), part)
    kept_counts = draw_kept_counts(jax.random.fold_in(arg_keys[5], 71), part)
    out_grad = noise(own_keys[4], (SEQS, LEN, D), 1.0, 6.0, ((0, 2), (2, 8)))
    return {"attended": attended, "weight_tiles": weight_tiles, "block_lists": block_lists, "kept_counts": kept_counts, "out_grad": out_grad}


def dense_weight(weight_tiles, block_lists, kept_counts):
    tensor_count, section_count, slot_count, tile_width, _ = weight_tiles.shape
    col_blocks = D // tile_width // N_TENSOR
    row_blocks = slot_count // col_blocks
    live = jnp.arange(slot_count)[None, None, :] < kept_counts[:, :, None]
    tiles = jnp.where(live[:, :, :, None, None], weight_tiles, jnp.zeros_like(weight_tiles))
    inverse = jnp.argsort(block_lists, axis=2).astype(jnp.int32)
    placed = jnp.take_along_axis(tiles, inverse[:, :, :, None, None], axis=2)
    placed = placed.reshape(tensor_count, section_count, row_blocks, col_blocks, tile_width, tile_width)
    placed = jnp.transpose(placed, (1, 2, 4, 0, 3, 5))
    return placed.reshape(section_count * row_blocks * tile_width, tensor_count * col_blocks * tile_width)


def reference(attended, weight_tiles, block_lists, kept_counts, out_grad):
    tensor_count, section_count, slot_count, tile_width, _ = weight_tiles.shape
    col_blocks = D // tile_width // N_TENSOR
    row_blocks = slot_count // col_blocks
    weight = dense_weight(weight_tiles, block_lists, kept_counts)
    in_width = attended.shape[2]

    def one_seq(running, pair):
        inputs, grads = pair
        output = jnp.dot(inputs, weight, preferred_element_type=jnp.float32).astype(jnp.bfloat16)
        grad_full = jnp.dot(inputs.T, grads, preferred_element_type=jnp.float32).astype(jnp.bfloat16)
        grad_full = lax.optimization_barrier(grad_full).astype(jnp.float32)
        return running + grad_full, output

    start = jnp.zeros((in_width, out_grad.shape[2]), jnp.float32)
    total, projected = lax.scan(one_seq, start, (attended, out_grad))
    blocks = total.reshape(section_count, row_blocks, tile_width, tensor_count, col_blocks, tile_width)
    blocks = jnp.transpose(blocks, (3, 0, 1, 4, 2, 5)).reshape(tensor_count, section_count, slot_count, tile_width, tile_width)
    picked = jnp.take_along_axis(blocks, block_lists.astype(jnp.int32)[:, :, :, None, None], axis=2)
    live = jnp.arange(slot_count)[None, None, :] < kept_counts[:, :, None]
    tiles_grad = jnp.where(live[:, :, :, None, None], picked, jnp.zeros_like(picked))
    return projected, tiles_grad
```

```python
import functools

import jax
import jax.numpy as jnp
from jax import lax
from jax.experimental import pallas as pl
from jax.experimental.pallas import tpu as pltpu
from jax.sharding import PartitionSpec as P

WEIGHTS = (6, 5, 3, 2)


def place_kernel(count, slot_ref, live_ref, *refs):
    tiles, out = refs[:count], refs[count]
    width = tiles[0].shape[-1]
    step = pl.program_id(0)
    for u in range(count):
        live = live_ref[step * count + u] > 0
        columns = slice(u * width, (u + 1) * width)

        @pl.when(live)
        def _():
            out[:, columns] = tiles[u][0]

        @pl.when(jnp.logical_not(live))
        def _():
            out[:, columns] = jnp.zeros_like(tiles[u][0])


def place_tiles(tiles, slot_of, live_of, row_blocks, col_blocks):
    width = tiles.shape[-1]
    count = min(8, col_blocks)
    groups = col_blocks // count

    def tile_map(u, i, slot_ref, live_ref):
        return (slot_ref[i * count + u], 0, 0)

    return pl.pallas_call(
        functools.partial(place_kernel, count),
        grid_spec=pltpu.PrefetchScalarGridSpec(
            num_scalar_prefetch=2,
            grid=(row_blocks * groups,),
            in_specs=[
                pl.BlockSpec((1, width, width), functools.partial(tile_map, u))
                for u in range(count)
            ],
            out_specs=pl.BlockSpec(
                (width, width * count), lambda i, s, l: (i // groups, i % groups)
            ),
        ),
        out_shape=jax.ShapeDtypeStruct(
            (row_blocks * width, col_blocks * width), tiles.dtype
        ),
        cost_estimate=pl.CostEstimate(
            flops=0, bytes_accessed=4 * tiles.size, transcendentals=0
        ),
        name="place",
    )(slot_of, live_of, *([tiles] * count))


def pick_kernel(count, block_ref, live_ref, *refs):
    blocks, out = refs[:count], refs[count]
    step = pl.program_id(0)
    for u in range(count):
        live = live_ref[step * count + u] > 0

        @pl.when(live)
        def _():
            out[u] = blocks[u][...]

        @pl.when(jnp.logical_not(live))
        def _():
            out[u] = jnp.zeros_like(blocks[u][...])


def pick_blocks(dense, block_of, live_of, width):
    slots = block_of.shape[0]
    col_blocks = dense.shape[1] // width
    count = 8 if slots % 8 == 0 else 1

    def block_map(u, i, block_ref, live_ref):
        block = block_ref[i * count + u]
        return (block // col_blocks, block % col_blocks)

    return pl.pallas_call(
        functools.partial(pick_kernel, count),
        grid_spec=pltpu.PrefetchScalarGridSpec(
            num_scalar_prefetch=2,
            grid=(slots // count,),
            in_specs=[
                pl.BlockSpec((width, width), functools.partial(block_map, u))
                for u in range(count)
            ],
            out_specs=pl.BlockSpec((count, width, width), lambda i, b, l: (i, 0, 0)),
        ),
        out_shape=jax.ShapeDtypeStruct((slots, width, width), dense.dtype),
        cost_estimate=pl.CostEstimate(
            flops=0, bytes_accessed=8 * slots * width * width, transcendentals=0
        ),
        name="pick",
    )(block_of, live_of, *([dense] * count))


def project_kernel(first, rows_ref, weight_ref, *refs):
    out = refs[-1]
    term = jnp.dot(rows_ref[...], weight_ref[...], preferred_element_type=jnp.float32)
    if not first:
        term = term + refs[0][...]
    out[...] = term.astype(out.dtype)


def project(rows, weight, partial, dtype, begin, height):
    depth, width = weight.shape
    block = min(512, height)
    offset = begin // block
    specs = [
        pl.BlockSpec((block, depth), lambda i: (offset + i, 0)),
        pl.BlockSpec((depth, width), lambda i: (0, 0)),
    ]
    args = [rows, weight]
    if partial is not None:
        specs.append(pl.BlockSpec((block, width), lambda i: (offset + i, 0)))
        args.append(partial)
    moved = (height * depth + depth * width) * 2 + height * width * 8
    return pl.pallas_call(
        functools.partial(project_kernel, partial is None),
        grid=(height // block,),
        in_specs=specs,
        out_specs=pl.BlockSpec((block, width), lambda i: (i, 0)),
        out_shape=jax.ShapeDtypeStruct((height, width), dtype),
        cost_estimate=pl.CostEstimate(
            flops=2 * height * depth * width, bytes_accessed=moved, transcendentals=0
        ),
        input_output_aliases=(
            {2: 0} if partial is not None and partial.dtype == dtype else {}
        ),
        compiler_params=pltpu.CompilerParams(vmem_limit_bytes=40 * 1024 * 1024),
        name="project",
    )(*args)


def combine_kernel(count, *refs):
    total = refs[0][...].astype(jnp.float32)
    for part in refs[1:count]:
        total = total + part[...].astype(jnp.float32)
    refs[-1][...] = total.astype(refs[-1].dtype)


def combine(parts, target, begin, length):
    height, width = parts[0].shape
    block = min(256, height)
    offset = begin // block
    specs = [pl.BlockSpec((block, width), lambda i: (i, 0))] * len(parts)
    args = list(parts)
    if target is not None:
        specs.append(pl.BlockSpec(memory_space=pl.ANY))
        args.append(target)
    return pl.pallas_call(
        functools.partial(combine_kernel, len(parts)),
        grid=(height // block,),
        in_specs=specs,
        out_specs=pl.BlockSpec((block, width), lambda i: (offset + i, 0)),
        out_shape=jax.ShapeDtypeStruct((length, width), parts[0].dtype),
        cost_estimate=pl.CostEstimate(
            flops=0, bytes_accessed=6 * height * width, transcendentals=0
        ),
        input_output_aliases={len(parts): 0} if target is not None else {},
        compiler_params=pltpu.CompilerParams(vmem_limit_bytes=40 * 1024 * 1024),
        name="combine",
    )(*args)


def shifted(x, axis, size, shift):
    return lax.ppermute(x, axis, [(i, (i + shift) % size) for i in range(size)])


def local(n_tensor, n_section, n_dp, attended, weight_tiles, block_lists, kept_counts, out_grad):
    width = weight_tiles.shape[-1]
    slots = weight_tiles.shape[2]
    rows, in_width = attended.shape[1:]
    row_blocks = in_width // width
    col_blocks = slots // row_blocks
    out_width = col_blocks * width
    total = sum(WEIGHTS)
    edges = [row_blocks * sum(WEIGHTS[:i]) // total for i in range(len(WEIGHTS) + 1)]
    spans = [(a * width, b * width) for a, b in zip(edges, edges[1:]) if b > a]

    own = out_grad[0]
    if n_section == 2:
        other = shifted(own, "section", 2, 1)
        first = lax.axis_index("section") == 0
        columns = jnp.concatenate(
            [jnp.where(first, own, other), jnp.where(first, other, own)], axis=1
        )
    else:
        columns = lax.all_gather(own, "section", axis=1, tiled=True)

    places = block_lists[0, 0]
    numbers = jnp.arange(slots, dtype=jnp.int32)
    slot_of = jnp.sum(
        jnp.where(places[None, :] == numbers[:, None], numbers[None, :], 0), axis=1
    )
    count = kept_counts[0, 0]
    live_of = (slot_of < count).astype(jnp.int32)
    weight = place_tiles(
        weight_tiles[0, 0], jnp.where(live_of > 0, slot_of, 0), live_of, row_blocks, col_blocks
    )

    pieces = [attended[0, :, lo:hi] for lo, hi in spans]
    arrived = []
    for number, piece in enumerate(pieces):
        if number == 1:
            piece, arrived[0] = lax.optimization_barrier((piece, arrived[0]))
        elif number > 1:
            piece, arrived[number - 2] = lax.optimization_barrier((piece, arrived[number - 2]))
        arrived.append(lax.all_gather(piece, "tensor", axis=0))

    length = n_tensor * rows
    partial = None
    mine = []
    sums = jnp.zeros((in_width, out_width), jnp.float32)
    for number, (lo, hi) in enumerate(spans):
        flat = arrived[number].reshape(length, hi - lo)
        grad = lax.dot_general(
            flat, columns, (((0,), (0,)), ((), ())), preferred_element_type=jnp.float32
        ).astype(jnp.bfloat16)
        flat, grad = lax.optimization_barrier((flat, grad))
        summed = grad.astype(jnp.float32)
        for shift in range(1, n_dp):
            summed = summed + shifted(grad, "dp", n_dp, shift).astype(jnp.float32)
        sums = lax.dynamic_update_slice(sums, summed, (lo, 0))
        part = weight[lo:hi]
        if number + 1 < len(spans):
            partial = project(flat, part, partial, jnp.float32, 0, length)
            if number + 2 < len(spans):
                later = number + 1
                arrived[later], partial = lax.optimization_barrier((arrived[later], partial))
        else:
            quarter = length // 4
            mine = [
                project(flat, part, partial, jnp.bfloat16, q * quarter, quarter)
                for q in range(4)
            ]

    projected = None
    for q, own_part in enumerate(mine):
        parts = [own_part] + [
            shifted(own_part, "section", n_section, shift) for shift in range(1, n_section)
        ]
        projected = combine(parts, projected, q * (length // 4), length)

    share = slots // n_dp
    start = lax.axis_index("dp") * share
    mine = lax.dynamic_slice(places, (start,), (share,))
    live = ((start + jnp.arange(share, dtype=jnp.int32)) < count).astype(jnp.int32)
    tiles_grad = pick_blocks(sums, jnp.where(live > 0, mine, 0), live, width)
    return (projected[None], tiles_grad[None, None])


def solution(mesh):
    in_specs = (
        P(("groups", "dp"), "tensor", "section"),
        P("tensor", "section", None, None, None),
        P("tensor", "section", None),
        P("tensor", "section"),
        P(("groups", "dp"), None, ("tensor", "section")),
    )
    out_specs = (
        P(("groups", "dp"), None, "tensor"),
        P(("groups", "tensor"), "section", "dp", None, None),
    )
    body = functools.partial(
        local, mesh.shape["tensor"], mesh.shape["section"], mesh.shape["dp"]
    )
    return jax.shard_map(body, mesh=mesh, in_specs=in_specs, out_specs=out_specs, check_vma=False)
```

```python
import functools
import math

import jax
import jax.numpy as jnp
from jax import lax
from jax.experimental import pallas as pl
from jax.experimental.pallas import tpu as pltpu
from jax.sharding import PartitionSpec as P

WEIGHTS = (5, 5, 4, 2)
SMALL = pl.CostEstimate(flops=0, bytes_accessed=1024, transcendentals=0)


def place_kernel(count, first, slot_ref, live_ref, *refs):
    tiles, out = refs[:count], refs[count]
    width = tiles[0].shape[-1]
    step = pl.program_id(0)
    for u in range(count):
        live = live_ref[first + step * count + u] > 0
        columns = slice(u * width, (u + 1) * width)

        @pl.when(live)
        def _():
            out[:, columns] = tiles[u][0]

        @pl.when(jnp.logical_not(live))
        def _():
            out[:, columns] = jnp.zeros_like(tiles[u][0])


def place_tiles(tiles, slot_of, live_of, row_begin, row_blocks, col_blocks):
    width = tiles.shape[-1]
    count = min(8, col_blocks)
    groups = col_blocks // count
    first = row_begin * col_blocks

    def tile_map(u, i, slot_ref, live_ref):
        return (slot_ref[first + i * count + u], 0, 0)

    return pl.pallas_call(
        functools.partial(place_kernel, count, first),
        grid_spec=pltpu.PrefetchScalarGridSpec(
            num_scalar_prefetch=2,
            grid=(row_blocks * groups,),
            in_specs=[
                pl.BlockSpec((1, width, width), functools.partial(tile_map, u))
                for u in range(count)
            ],
            out_specs=pl.BlockSpec(
                (width, width * count), lambda i, s, l: (i // groups, i % groups)
            ),
        ),
        out_shape=jax.ShapeDtypeStruct(
            (row_blocks * width, col_blocks * width), tiles.dtype
        ),
        cost_estimate=SMALL,
        name="place",
    )(slot_of, live_of, *([tiles] * count))


def pick_kernel(count, block_ref, live_ref, *refs):
    blocks, out = refs[:count], refs[count]
    step = pl.program_id(0)
    for u in range(count):
        live = live_ref[step * count + u] > 0

        @pl.when(live)
        def _():
            out[u] = blocks[u][...]

        @pl.when(jnp.logical_not(live))
        def _():
            out[u] = jnp.zeros_like(blocks[u][...])


def pick_blocks(dense, block_of, live_of, width):
    slots = block_of.shape[0]
    col_blocks = dense.shape[1] // width
    count = 8 if slots % 8 == 0 else 1

    def block_map(u, i, block_ref, live_ref):
        block = block_ref[i * count + u]
        return (block // col_blocks, block % col_blocks)

    return pl.pallas_call(
        functools.partial(pick_kernel, count),
        grid_spec=pltpu.PrefetchScalarGridSpec(
            num_scalar_prefetch=2,
            grid=(slots // count,),
            in_specs=[
                pl.BlockSpec((width, width), functools.partial(block_map, u))
                for u in range(count)
            ],
            out_specs=pl.BlockSpec((count, width, width), lambda i, b, l: (i, 0, 0)),
        ),
        out_shape=jax.ShapeDtypeStruct((slots, width, width), dense.dtype),
        cost_estimate=SMALL,
        name="pick",
    )(block_of, live_of, *([dense] * count))


def project_kernel(first, rows_ref, weight_ref, *refs):
    out = refs[-1]
    term = jnp.dot(rows_ref[...], weight_ref[...], preferred_element_type=jnp.float32)
    if not first:
        term = term + refs[0][...]
    out[...] = term.astype(out.dtype)


def project(rows, weight, partial, dtype, begin, height):
    depth, width = weight.shape
    block = min(512, height)
    offset = begin // block
    specs = [
        pl.BlockSpec((block, depth), lambda i: (offset + i, 0)),
        pl.BlockSpec((depth, width), lambda i: (0, 0)),
    ]
    args = [rows, weight]
    if partial is not None:
        specs.append(pl.BlockSpec((block, width), lambda i: (offset + i, 0)))
        args.append(partial)
    cost = pl.CostEstimate(
        flops=2 * height * depth * width,
        bytes_accessed=(height * depth + depth * width) * 2 + height * width * 8,
        transcendentals=0,
    )
    return pl.pallas_call(
        functools.partial(project_kernel, partial is None),
        grid=(height // block,),
        in_specs=specs,
        out_specs=pl.BlockSpec((block, width), lambda i: (i, 0)),
        out_shape=jax.ShapeDtypeStruct((height, width), dtype),
        cost_estimate=SMALL,
        input_output_aliases=(
            {2: 0} if partial is not None and partial.dtype == dtype else {}
        ),
        compiler_params=pltpu.CompilerParams(vmem_limit_bytes=40 * 1024 * 1024),
        name="project",
    )(*args)


def combine_kernel(count, *refs):
    total = refs[0][...].astype(jnp.float32)
    for part in refs[1:count]:
        total = total + part[...].astype(jnp.float32)
    refs[-1][...] = total.astype(refs[-1].dtype)


def combine(parts, target, begin, length, dtype):
    height, width = parts[0].shape
    block = math.gcd(math.gcd(256, height), begin)
    offset = begin // block
    specs = [pl.BlockSpec((block, width), lambda i: (i, 0))] * len(parts)
    args = list(parts)
    if target is not None:
        specs.append(pl.BlockSpec(memory_space=pl.ANY))
        args.append(target)
    return pl.pallas_call(
        functools.partial(combine_kernel, len(parts)),
        grid=(height // block,),
        in_specs=specs,
        out_specs=pl.BlockSpec((block, width), lambda i: (offset + i, 0)),
        out_shape=jax.ShapeDtypeStruct((length, width), dtype),
        cost_estimate=SMALL,
        input_output_aliases={len(parts): 0} if target is not None else {},
        compiler_params=pltpu.CompilerParams(vmem_limit_bytes=40 * 1024 * 1024),
        name="combine",
    )(*args)


def shifted(x, axis, size, shift):
    return lax.ppermute(x, axis, [(i, (i + shift) % size) for i in range(size)])


def local(n_tensor, n_section, n_dp, attended, weight_tiles, block_lists, kept_counts, out_grad):
    width = weight_tiles.shape[-1]
    slots = weight_tiles.shape[2]
    rows, in_width = attended.shape[1:]
    row_blocks = in_width // width
    col_blocks = slots // row_blocks
    out_width = col_blocks * width
    total = sum(WEIGHTS)
    edges = [row_blocks * sum(WEIGHTS[:i]) // total for i in range(len(WEIGHTS) + 1)]
    spans = [(a * width, b * width) for a, b in zip(edges, edges[1:]) if b > a]

    own = out_grad[0]
    if n_section == 2:
        other = shifted(own, "section", 2, 1)
        first = lax.axis_index("section") == 0
        columns = jnp.concatenate(
            [jnp.where(first, own, other), jnp.where(first, other, own)], axis=1
        )
    else:
        columns = lax.all_gather(own, "section", axis=1, tiled=True)

    places = block_lists[0, 0]
    numbers = jnp.arange(slots, dtype=jnp.int32)
    slot_of = jnp.sum(
        jnp.where(places[None, :] == numbers[:, None], numbers[None, :], 0), axis=1
    )
    count = kept_counts[0, 0]
    live_of = (slot_of < count).astype(jnp.int32)
    placed_slot = jnp.where(live_of > 0, slot_of, 0)
    weights = [
        place_tiles(
            weight_tiles[0, 0], placed_slot, live_of, lo // width, (hi - lo) // width, col_blocks
        )
        for lo, hi in spans
    ]

    pieces = [attended[0, :, lo:hi] for lo, hi in spans]
    arrived = []
    for number, piece in enumerate(pieces):
        if number == 1:
            piece, arrived[0] = lax.optimization_barrier((piece, arrived[0]))
        elif number > 1:
            piece, arrived[number - 2] = lax.optimization_barrier((piece, arrived[number - 2]))
        arrived.append(lax.all_gather(piece, "tensor", axis=0))

    length = n_tensor * rows
    partial = None
    mine = []
    sums = None
    for number, (lo, hi) in enumerate(spans):
        flat = arrived[number].reshape(length, hi - lo)
        grad = lax.dot_general(
            flat, columns, (((0,), (0,)), ((), ())), preferred_element_type=jnp.float32
        ).astype(jnp.bfloat16)
        flat, grad = lax.optimization_barrier((flat, grad))
        parts = [grad] + [shifted(grad, "dp", n_dp, shift) for shift in range(1, n_dp)]
        sums = combine(parts, sums, lo, in_width, jnp.float32)
        if number == len(spans) - 3:
            arrived[-1], sums = lax.optimization_barrier((arrived[-1], sums))
        part = weights[number]
        if number + 1 < len(spans):
            partial = project(flat, part, partial, jnp.float32, 0, length)
            if number + 2 < len(spans):
                later = number + 1
                arrived[later], partial = lax.optimization_barrier((arrived[later], partial))
        else:
            quarter = length // 4
            mine = [
                project(flat, part, partial, jnp.bfloat16, q * quarter, quarter)
                for q in range(4)
            ]

    projected = None
    for q, own_part in enumerate(mine):
        parts = [own_part] + [
            shifted(own_part, "section", n_section, shift) for shift in range(1, n_section)
        ]
        projected = combine(parts, projected, q * (length // 4), length, jnp.bfloat16)

    share = slots // n_dp
    start = lax.axis_index("dp") * share
    mine = lax.dynamic_slice(places, (start,), (share,))
    live = ((start + jnp.arange(share, dtype=jnp.int32)) < count).astype(jnp.int32)
    tiles_grad = pick_blocks(sums, jnp.where(live > 0, mine, 0), live, width)
    return (projected[None], tiles_grad[None, None])


def solution(mesh):
    in_specs = (
        P(("groups", "dp"), "tensor", "section"),
        P("tensor", "section", None, None, None),
        P("tensor", "section", None),
        P("tensor", "section"),
        P(("groups", "dp"), None, ("tensor", "section")),
    )
    out_specs = (
        P(("groups", "dp"), None, "tensor"),
        P(("groups", "tensor"), "section", "dp", None, None),
    )
    body = functools.partial(
        local, mesh.shape["tensor"], mesh.shape["section"], mesh.shape["dp"]
    )
    return jax.shard_map(body, mesh=mesh, in_specs=in_specs, out_specs=out_specs, check_vma=False)
```

```python
import functools
import math

import jax
import jax.numpy as jnp
from jax import lax
from jax.experimental import pallas as pl
from jax.experimental.pallas import tpu as pltpu
from jax.sharding import PartitionSpec as P

WEIGHTS = (5, 5, 4, 2)
SMALL = pl.CostEstimate(flops=0, bytes_accessed=1024, transcendentals=0)


def place_kernel(count, first, slot_ref, live_ref, *refs):
    tiles, out = refs[:count], refs[count]
    width = tiles[0].shape[-1]
    step = pl.program_id(0)
    for u in range(count):
        live = live_ref[first + step * count + u] > 0
        columns = slice(u * width, (u + 1) * width)

        @pl.when(live)
        def _():
            out[:, columns] = tiles[u][0]

        @pl.when(jnp.logical_not(live))
        def _():
            out[:, columns] = jnp.zeros_like(tiles[u][0])


def place_tiles(tiles, slot_of, live_of, row_begin, row_blocks, col_blocks):
    width = tiles.shape[-1]
    count = min(8, col_blocks)
    groups = col_blocks // count
    first = row_begin * col_blocks

    def tile_map(u, i, slot_ref, live_ref):
        return (slot_ref[first + i * count + u], 0, 0)

    return pl.pallas_call(
        functools.partial(place_kernel, count, first),
        grid_spec=pltpu.PrefetchScalarGridSpec(
            num_scalar_prefetch=2,
            grid=(row_blocks * groups,),
            in_specs=[
                pl.BlockSpec((1, width, width), functools.partial(tile_map, u))
                for u in range(count)
            ],
            out_specs=pl.BlockSpec(
                (width, width * count), lambda i, s, l: (i // groups, i % groups)
            ),
        ),
        out_shape=jax.ShapeDtypeStruct(
            (row_blocks * width, col_blocks * width), tiles.dtype
        ),
        cost_estimate=SMALL,
        name="place",
    )(slot_of, live_of, *([tiles] * count))


def pick_kernel(count, block_ref, live_ref, *refs):
    blocks, out = refs[:count], refs[count]
    step = pl.program_id(0)
    for u in range(count):
        live = live_ref[step * count + u] > 0

        @pl.when(live)
        def _():
            out[u] = blocks[u][...]

        @pl.when(jnp.logical_not(live))
        def _():
            out[u] = jnp.zeros_like(blocks[u][...])


def pick_blocks(dense, block_of, live_of, width):
    slots = block_of.shape[0]
    col_blocks = dense.shape[1] // width
    count = 8 if slots % 8 == 0 else 1

    def block_map(u, i, block_ref, live_ref):
        block = block_ref[i * count + u]
        return (block // col_blocks, block % col_blocks)

    return pl.pallas_call(
        functools.partial(pick_kernel, count),
        grid_spec=pltpu.PrefetchScalarGridSpec(
            num_scalar_prefetch=2,
            grid=(slots // count,),
            in_specs=[
                pl.BlockSpec((width, width), functools.partial(block_map, u))
                for u in range(count)
            ],
            out_specs=pl.BlockSpec((count, width, width), lambda i, b, l: (i, 0, 0)),
        ),
        out_shape=jax.ShapeDtypeStruct((slots, width, width), dense.dtype),
        cost_estimate=SMALL,
        name="pick",
    )(block_of, live_of, *([dense] * count))


def project_kernel(first, rows_ref, weight_ref, *refs):
    out = refs[-1]
    term = jnp.dot(rows_ref[...], weight_ref[...], preferred_element_type=jnp.float32)
    if not first:
        term = term + refs[0][...]
    out[...] = term.astype(out.dtype)


def project(rows, weight, partial, dtype, begin, height):
    depth, width = weight.shape
    block = min(512, height)
    offset = begin // block
    specs = [
        pl.BlockSpec((block, depth), lambda i: (offset + i, 0)),
        pl.BlockSpec((depth, width), lambda i: (0, 0)),
    ]
    args = [rows, weight]
    if partial is not None:
        specs.append(pl.BlockSpec((block, width), lambda i: (offset + i, 0)))
        args.append(partial)
    cost = pl.CostEstimate(
        flops=2 * height * depth * width,
        bytes_accessed=(height * depth + depth * width) * 2 + height * width * 8,
        transcendentals=0,
    )
    return pl.pallas_call(
        functools.partial(project_kernel, partial is None),
        grid=(height // block,),
        in_specs=specs,
        out_specs=pl.BlockSpec((block, width), lambda i: (i, 0)),
        out_shape=jax.ShapeDtypeStruct((height, width), dtype),
        cost_estimate=SMALL,
        input_output_aliases=(
            {2: 0} if partial is not None and partial.dtype == dtype else {}
        ),
        compiler_params=pltpu.CompilerParams(vmem_limit_bytes=40 * 1024 * 1024),
        name="project",
    )(*args)


def combine_kernel(count, *refs):
    total = refs[0][...].astype(jnp.float32)
    for part in refs[1:count]:
        total = total + part[...].astype(jnp.float32)
    refs[-1][...] = total.astype(refs[-1].dtype)


def combine(parts, target, begin, length, dtype):
    height, width = parts[0].shape
    block = math.gcd(math.gcd(256, height), begin)
    offset = begin // block
    specs = [pl.BlockSpec((block, width), lambda i: (i, 0))] * len(parts)
    args = list(parts)
    if target is not None:
        specs.append(pl.BlockSpec(memory_space=pl.ANY))
        args.append(target)
    return pl.pallas_call(
        functools.partial(combine_kernel, len(parts)),
        grid=(height // block,),
        in_specs=specs,
        out_specs=pl.BlockSpec((block, width), lambda i: (offset + i, 0)),
        out_shape=jax.ShapeDtypeStruct((length, width), dtype),
        cost_estimate=SMALL,
        input_output_aliases={len(parts): 0} if target is not None else {},
        compiler_params=pltpu.CompilerParams(vmem_limit_bytes=40 * 1024 * 1024),
        name="combine",
    )(*args)


def shifted(x, axis, size, shift):
    return lax.ppermute(x, axis, [(i, (i + shift) % size) for i in range(size)])


def local(n_tensor, n_section, n_dp, attended, weight_tiles, block_lists, kept_counts, out_grad):
    width = weight_tiles.shape[-1]
    slots = weight_tiles.shape[2]
    rows, in_width = attended.shape[1:]
    row_blocks = in_width // width
    col_blocks = slots // row_blocks
    out_width = col_blocks * width
    total = sum(WEIGHTS)
    edges = [row_blocks * sum(WEIGHTS[:i]) // total for i in range(len(WEIGHTS) + 1)]
    spans = [(a * width, b * width) for a, b in zip(edges, edges[1:]) if b > a]

    own = out_grad[0]
    if n_section == 2:
        other = shifted(own, "section", 2, 1)
        first = lax.axis_index("section") == 0
        columns = jnp.concatenate(
            [jnp.where(first, own, other), jnp.where(first, other, own)], axis=1
        )
    else:
        columns = lax.all_gather(own, "section", axis=1, tiled=True)

    places = block_lists[0, 0]
    numbers = jnp.arange(slots, dtype=jnp.int32)
    slot_of = jnp.sum(
        jnp.where(places[None, :] == numbers[:, None], numbers[None, :], 0), axis=1
    )
    count = kept_counts[0, 0]
    live_of = (slot_of < count).astype(jnp.int32)
    placed_slot = jnp.where(live_of > 0, slot_of, 0)
    weights = [
        place_tiles(
            weight_tiles[0, 0], placed_slot, live_of, lo // width, (hi - lo) // width, col_blocks
        )
        for lo, hi in spans
    ]

    pieces = [attended[0, :, lo:hi] for lo, hi in spans]
    arrived = []
    for number, piece in enumerate(pieces):
        if number == 1:
            piece, arrived[0] = lax.optimization_barrier((piece, arrived[0]))
        elif number > 1:
            piece, arrived[number - 2] = lax.optimization_barrier((piece, arrived[number - 2]))
        arrived.append(lax.all_gather(piece, "tensor", axis=0))

    length = n_tensor * rows
    partial = None
    mine = []
    sums = None
    for number, (lo, hi) in enumerate(spans):
        flat = arrived[number].reshape(length, hi - lo)
        grad = lax.dot_general(
            flat, columns, (((0,), (0,)), ((), ())), preferred_element_type=jnp.float32
        ).astype(jnp.bfloat16)
        flat, grad = lax.optimization_barrier((flat, grad))
        parts = [grad] + [shifted(grad, "dp", n_dp, shift) for shift in range(1, n_dp)]
        if number + 1 == len(spans) and number > 0:
            flat, sums = lax.optimization_barrier((flat, sums))
        else:
            sums = combine(parts, sums, lo, in_width, jnp.float32)
        if number == len(spans) - 3:
            arrived[-1], sums = lax.optimization_barrier((arrived[-1], sums))
        part = weights[number]
        if number + 1 < len(spans):
            partial = project(flat, part, partial, jnp.float32, 0, length)
            if number + 2 < len(spans):
                later = number + 1
                arrived[later], partial = lax.optimization_barrier((arrived[later], partial))
        else:
            quarter = length // 4
            mine = [
                project(flat, part, partial, jnp.bfloat16, q * quarter, quarter)
                for q in range(4)
            ]

    last_parts = parts
    projected = None
    for q, own_part in enumerate(mine):
        parts = [own_part] + [
            shifted(own_part, "section", n_section, shift) for shift in range(1, n_section)
        ]
        projected = combine(parts, projected, q * (length // 4), length, jnp.bfloat16)
        if q == 2 and len(spans) > 1:
            parts_here, projected = lax.optimization_barrier((last_parts[0], projected))
            sums = combine(
                [parts_here] + last_parts[1:], sums, spans[-1][0], in_width, jnp.float32
            )

    share = slots // n_dp
    start = lax.axis_index("dp") * share
    mine = lax.dynamic_slice(places, (start,), (share,))
    live = ((start + jnp.arange(share, dtype=jnp.int32)) < count).astype(jnp.int32)
    tiles_grad = pick_blocks(sums, jnp.where(live > 0, mine, 0), live, width)
    return (projected[None], tiles_grad[None, None])


def solution(mesh):
    in_specs = (
        P(("groups", "dp"), "tensor", "section"),
        P("tensor", "section", None, None, None),
        P("tensor", "section", None),
        P("tensor", "section"),
        P(("groups", "dp"), None, ("tensor", "section")),
    )
    out_specs = (
        P(("groups", "dp"), None, "tensor"),
        P(("groups", "tensor"), "section", "dp", None, None),
    )
    body = functools.partial(
        local, mesh.shape["tensor"], mesh.shape["section"], mesh.shape["dp"]
    )
    return jax.shard_map(body, mesh=mesh, in_specs=in_specs, out_specs=out_specs, check_vma=False)
```
